256 devices in a mesh: img: 64 (over y_lo, x, z), head: 4 (over y_hi, core).
Axes of the slice: x: 4, y: 4 (y_hi: 2, y_lo: 2; y = y_hi * 2 + y_lo), z: 8, core: 2. Of those that a mesh axis runs over, the one named last changes fastest.
Arguments:
- inputs: bfloat16 [16384, 1280], P('img'), may hold values from -16 to 16
- middle: bfloat16 [16384, 1280], P('img'), may hold values from -16 to 16
- out_grad: bfloat16 [16384, 1280], P('img'), may hold values from -16 to 16
- cached_maps: bfloat16 [64, 16, 256, 256], P('img', 'head'), may hold values from 0 to 1, as said below
- w_value: bfloat16 [1280, 1280], P(None, 'head'), may hold values from -0.15625 to 0.15625
- w_out: bfloat16 [1280, 1280], P('head'), may hold values from -0.15625 to 0.15625
- w_up: bfloat16 [1280, 2560], P(None, 'head'), may hold values from -0.15625 to 0.15625
- w_down: bfloat16 [2560, 1280], P('head'), may hold values from -0.125 to 0.125
Outputs:
- in_grad: bfloat16 [16384, 1280], P(('img', 'head'))
- grad_value: float32 [1280, 1280], P('img', 'head')
- grad_out: float32 [1280, 1280], P('head', 'img')
- grad_up: float32 [1280, 2560], P('img', 'head')
- grad_down: float32 [2560, 1280], P('head', 'img')
The draws below stay inside these ranges and needn't reach their ends.
Inputs may be any that keep to these rules, and one draw needn't show every extreme that they name: `cached_maps`: every row of every map is positive and sums to one up to rounding.
All inputs are finite; a program needn't handle non-finite values.
Results may differ from the reference program's by a relative error of at most 0.0069.
Values may be sent and summed in bfloat16 or wider, within the bound.
No kernel may reach another device: no remote copies, remote signals or barrier semaphores. Data moves between devices by JAX's collectives and lax.ppermute only.
A program may use at most 128 MiB of HBM per device.

```python
import jax
import jax.numpy as jnp
from jax import lax

D = 1280
FF = 2560
HEADS = 16
TOK = 256
HDIM = 80
IMAGES = 64


def draw_cached_maps(key, part):
    first_key, second_key = jax.random.split(jax.random.fold_in(key, 7))
    sharpness = jnp.exp(jax.random.uniform(first_key, (IMAGES, HEADS, 1, 1), jnp.float32, -0.7, 1.4))
    logits = jax.random.normal(second_key, (IMAGES, HEADS, TOK, TOK), jnp.float32)
    return jax.nn.softmax(logits * sharpness, axis=-1).astype(jnp.bfloat16)


def strengthened(array, rng, source, target, parts, factor):
    owner, partner = [(jnp.arange(array.shape[axis_at]) // (array.shape[axis_at] // parts)).reshape([-1 if axis == axis_at else 1 for axis in range(array.ndim)]) for axis_at in (source, target)]
    chosen = jax.random.permutation(rng, parts)[partner]
    strong = (owner == chosen) | (owner == (partner + parts // 2) % parts)
    return jnp.where(strong, factor * array, array)


def steps_of(own_key, extent, pieces, low, top_value):
    def one(position, blocks):
        steps = jax.random.uniform(jax.random.fold_in(jax.random.fold_in(own_key, 6), position), (blocks,), jnp.float32, low / len(pieces), top_value / len(pieces))
        return jnp.repeat(jnp.exp(steps), extent[position] // blocks).reshape((-1,) + (1,) * (len(extent) - position - 1))

    level = one(*pieces[0])
    for cut in pieces[1:]:
        level = level * one(*cut)
    return level


def noise(own_key, dims, width, bound, pieces=(), kind=jnp.bfloat16):
    values = width * jax.random.normal(own_key, dims, jnp.float32)
    if pieces:
        values = values * steps_of(own_key, dims, pieces, -0.22, 0.18)
    return jnp.clip(values, -bound, bound).astype(kind)


def noise_with(stream_key, extent, scale, reach, cuts, heavy, dtype=jnp.bfloat16):
    drawn = scale * jax.random.normal(stream_key, extent, jnp.float32)
    if cuts:
        drawn = drawn * steps_of(stream_key, extent, cuts, -0.22, 0.18)
    return jnp.clip(strengthened(drawn, jax.random.fold_in(stream_key, 3), *heavy), -reach, reach).astype(dtype)


def setup_inputs(seed: int = 0) -> dict:
    key_of = jax.random.split(jax.random.key(seed), 9)
    inputs = noise_with(key_of[0], (IMAGES * TOK, D), 1.0, 16.0, ((0, 64),), (0, 1, 64, 4.0))
    middle = noise_with(key_of[1], (IMAGES * TOK, D), 1.0, 16.0, ((0, 64),), (0, 1, 64, 4.0))
    out_grad = noise_with(key_of[2], (IMAGES * TOK, D), 1.0, 16.0, ((0, 64),), (0, 1, 64, 4.0))
    cached_maps = draw_cached_maps(jax.random.fold_in(key_of[8], 71), 0)
    w_value = noise(key_of[4], (D, D), D ** -0.5, 0.15625, ((1, 4),))
    w_out = noise(key_of[5], (D, D), D ** -0.5, 0.15625, ((0, 4),))
    w_up = noise(key_of[6], (D, FF), D ** -0.5, 0.15625, ((1, 4),))
    w_down = noise(key_of[7], (FF, D), FF ** -0.5, 0.125, ((0, 4),))
    return {"inputs": inputs, "middle": middle, "out_grad": out_grad, "cached_maps": cached_maps, "w_value": w_value, "w_out": w_out, "w_up": w_up, "w_down": w_down}


def norm_rows(rows):
    centre = rows - lax.optimization_barrier(jnp.mean(rows, axis=-1, keepdims=True))
    spread = lax.optimization_barrier(jnp.mean(centre * centre, axis=-1, keepdims=True))
    return centre * lax.rsqrt(spread + 1e-06)

def norm_back(rows, grad):
    centre = rows - lax.optimization_barrier(jnp.mean(rows, axis=-1, keepdims=True))
    factor = lax.rsqrt(lax.optimization_barrier(jnp.mean(centre * centre, axis=-1, keepdims=True)) + 1e-06)
    normed = centre * factor
    return factor * (grad - lax.optimization_barrier(jnp.mean(grad, axis=-1, keepdims=True)) - normed * lax.optimization_barrier(jnp.mean(grad * normed, axis=-1, keepdims=True)))

def gelu_tanh(pre):
    return jax.nn.gelu(pre, approximate=True)

def reference(inputs, middle, out_grad, cached_maps, w_value, w_out, w_up, w_down):
    inputs_all = inputs.reshape(IMAGES, TOK, D)
    middle_all = middle.reshape(IMAGES, TOK, D)
    grads_all = out_grad.reshape(IMAGES, TOK, D)

    def one_image(totals, item):
        source, saved, upstream, maps_one = item
        source_f = source.astype(jnp.float32)
        saved_f = saved.astype(jnp.float32)
        normed_in = norm_rows(source_f).astype(jnp.bfloat16)
        values = jnp.dot(normed_in, w_value, preferred_element_type=jnp.float32).astype(jnp.bfloat16)
        maps_f = maps_one.astype(jnp.float32)
        attended = jnp.einsum('htk,khd->thd', maps_f, values.reshape(TOK, HEADS, HDIM).astype(jnp.float32))
        attended = attended.astype(jnp.bfloat16).reshape(TOK, D)
        normed_mid = norm_rows(saved_f).astype(jnp.bfloat16)
        pre = jnp.dot(normed_mid, w_up, preferred_element_type=jnp.float32)
        hidden = gelu_tanh(pre).astype(jnp.bfloat16)
        hidden_grad = jnp.dot(upstream, w_down.T, preferred_element_type=jnp.float32)
        pre_grad = jax.vjp(gelu_tanh, pre)[1](hidden_grad)[0].astype(jnp.bfloat16)
        grad_down = jnp.dot(hidden.T, upstream, preferred_element_type=jnp.float32)
        grad_up = jnp.dot(normed_mid.T, pre_grad, preferred_element_type=jnp.float32)
        mid_grad = upstream.astype(jnp.float32) + norm_back(saved_f, jnp.dot(pre_grad, w_up.T, preferred_element_type=jnp.float32))
        mid_grad_b = mid_grad.astype(jnp.bfloat16)
        grad_out = jnp.dot(attended.T, mid_grad_b, preferred_element_type=jnp.float32)
        att_grad = jnp.dot(mid_grad_b, w_out.T, preferred_element_type=jnp.float32).astype(jnp.bfloat16)
        value_grad = jnp.einsum('htk,thd->khd', maps_f, att_grad.reshape(TOK, HEADS, HDIM).astype(jnp.float32))
        value_grad = value_grad.astype(jnp.bfloat16).reshape(TOK, D)
        grad_value = jnp.dot(normed_in.T, value_grad, preferred_element_type=jnp.float32)
        in_grad = mid_grad + norm_back(source_f, jnp.dot(value_grad, w_value.T, preferred_element_type=jnp.float32))
        totals = (totals[0] + grad_value, totals[1] + grad_out, totals[2] + grad_up, totals[3] + grad_down)
        return (totals, in_grad.astype(jnp.bfloat16))
    start = (jnp.zeros((D, D), jnp.float32), jnp.zeros((D, D), jnp.float32), jnp.zeros((D, FF), jnp.float32), jnp.zeros((FF, D), jnp.float32))
    totals, in_grads = lax.scan(one_image, start, (inputs_all, middle_all, grads_all, cached_maps))
    return (in_grads.reshape(IMAGES * TOK, D), totals[0], totals[1], totals[2], totals[3])
```

```python
import jax
import jax.numpy as jnp
from jax import lax
from jax.sharding import Mesh, PartitionSpec as P

SIZE = {"yl": 2, "x": 4, "z": 8, "yh": 2, "core": 2}
BF = jnp.bfloat16
F32 = jnp.float32


def norm_rows(rows):
    centre = rows - jnp.mean(rows, axis=-1, keepdims=True)
    spread = jnp.mean(centre * centre, axis=-1, keepdims=True)
    return centre * lax.rsqrt(spread + 1e-06)


def norm_back(rows, grad):
    centre = rows - jnp.mean(rows, axis=-1, keepdims=True)
    factor = lax.rsqrt(jnp.mean(centre * centre, axis=-1, keepdims=True) + 1e-06)
    normed = centre * factor
    return factor * (
        grad
        - jnp.mean(grad, axis=-1, keepdims=True)
        - normed * jnp.mean(grad * normed, axis=-1, keepdims=True)
    )


def gelu_tanh(pre):
    return jax.nn.gelu(pre, approximate=True)


def shift(array, axis, by):
    n = SIZE[axis]
    return lax.ppermute(array, axis, [(i, (i + by) % n) for i in range(n)])


def pick(array, index, axis):
    return lax.dynamic_index_in_dim(array, index, axis, keepdims=False)


def sum_pair(term, axis, dim):
    me = lax.axis_index(axis)
    other = shift(pick(term, 1 - me, dim).astype(BF), axis, 1)
    return pick(term, me, dim).astype(F32) + other.astype(F32)


def sum_x(term, dim):
    me = lax.axis_index("x")
    total = pick(term, me, dim).astype(F32)
    for by in (2, 1, 3):
        part = shift(pick(term, (me + by) % 4, dim).astype(BF), "x", by)
        total = total + part.astype(F32)
    return total


def sum_z(term):
    cols = term.shape[-1]
    parts = lax.all_to_all(term.astype(BF).reshape(8, 20, cols), "z", 0, 0)
    return jnp.sum(parts.astype(F32), axis=0)


def x_first(term):
    cols = term.shape[-1]
    total = sum_x(term.reshape(2, 4, 160, cols), 1)
    return sum_pair(total, "yl", 0)


def y_first(term):
    cols = term.shape[-1]
    total = sum_pair(term.reshape(2, 640, cols), "yl", 0)
    return sum_x(total.reshape(4, 160, cols), 0)


def on_device(inputs, middle, out_grad, cached_maps, w_value, w_out, w_up, w_down):
    tok_rows = inputs.shape[0]
    heads_here = cached_maps.shape[1]
    core = lax.axis_index("core")
    yh = lax.axis_index("yh")
    maps_here = cached_maps[0]

    middle_f = middle.astype(F32)
    normed_mid = norm_rows(middle_f).astype(BF)
    pre = jnp.dot(normed_mid, w_up, preferred_element_type=F32)
    hidden = gelu_tanh(pre).astype(BF)
    hidden_grad = jnp.einsum("td,fd->tf", out_grad, w_down, preferred_element_type=F32)
    pre_grad = jax.vjp(gelu_tanh, pre)[1](hidden_grad)[0].astype(BF)
    mid_part = jnp.einsum("tf,df->td", pre_grad, w_up, preferred_element_type=F32)

    def mine(array):
        rows = array.reshape(2, 2, 64, -1)
        return pick(rows, core, 1).reshape(128, -1)

    mid_sum = sum_pair(mid_part.reshape(2, 2, 64, -1), "core", 1).reshape(128, -1)
    mid_sum_b = mid_sum.astype(BF)
    mid_sum = mid_sum + shift(mid_sum_b, "yh", 1).astype(F32)
    mid_mine = mine(out_grad).astype(F32) + norm_back(mine(middle).astype(F32), mid_sum)

    down_term = jnp.einsum("td,tf->df", out_grad, hidden, preferred_element_type=F32)
    up_term = jnp.einsum("tr,tf->rf", normed_mid, pre_grad, preferred_element_type=F32)
    down_sum = x_first(down_term)
    up_sum = y_first(up_term)

    normed_in = norm_rows(inputs.astype(F32)).astype(BF)
    values = jnp.dot(normed_in, w_value, preferred_element_type=F32).astype(BF)
    head_size = values.shape[1] // heads_here
    attended = jnp.einsum(
        "htk,khd->thd",
        maps_here,
        values.reshape(tok_rows, heads_here, head_size),
        preferred_element_type=F32,
    )
    attended = attended.astype(BF).reshape(tok_rows, -1)

    mid_b = mid_mine.astype(BF)
    other_b = shift(mid_b, "core", 1)
    both = jnp.stack([mid_b.reshape(2, 64, -1), other_b.reshape(2, 64, -1)], axis=1)
    swapped = jnp.stack([other_b.reshape(2, 64, -1), mid_b.reshape(2, 64, -1)], axis=1)
    mid_grad_b = jnp.where(core == 0, both, swapped).reshape(tok_rows, -1)

    att_grad = jnp.einsum("td,ed->te", mid_grad_b, w_out, preferred_element_type=F32).astype(BF)
    value_grad = jnp.einsum(
        "htk,thd->khd",
        maps_here,
        att_grad.reshape(tok_rows, heads_here, head_size),
        preferred_element_type=F32,
    )
    value_grad = value_grad.astype(BF).reshape(tok_rows, -1)
    input_part = jnp.einsum("te,de->td", value_grad, w_value, preferred_element_type=F32)
    outproj_term = jnp.einsum("td,te->de", mid_grad_b, attended, preferred_element_type=F32)
    value_term = jnp.einsum("tr,te->re", normed_in, value_grad, preferred_element_type=F32)

    in_sum = sum_pair(input_part.reshape(2, 2, 64, -1), "core", 1)
    in_sum = sum_pair(in_sum, "yh", 0)
    inputs_own = pick(pick(inputs.reshape(2, 2, 64, -1), yh, 0), core, 0).astype(F32)
    mid_own = pick(mid_mine.reshape(2, 64, -1), yh, 0)
    in_grad = (mid_own + norm_back(inputs_own, in_sum)).astype(BF)

    out_sum = x_first(outproj_term)
    value_sum = y_first(value_term)
    early = sum_z(jnp.concatenate([down_sum, up_sum], axis=1))
    late = sum_z(jnp.concatenate([out_sum, value_sum], axis=1))
    grad_down = early[:, : down_sum.shape[1]].T
    grad_up = early[:, down_sum.shape[1] :]
    grad_out = late[:, : out_sum.shape[1]].T
    grad_value = late[:, out_sum.shape[1] :]
    return (in_grad, grad_value, grad_out, grad_up, grad_down)


def solution(mesh):
    split = Mesh(mesh.devices.reshape(2, 4, 8, 2, 2), ("yl", "x", "z", "yh", "core"))
    img, head = ("yl", "x", "z"), ("yh", "core")
    return jax.shard_map(
        on_device,
        mesh=split,
        in_specs=(
            P(img, None),
            P(img, None),
            P(img, None),
            P(img, head, None, None),
            P(None, head),
            P(head, None),
            P(None, head),
            P(head, None),
        ),
        out_specs=(
            P(img + head, None),
            P(img, head),
            P(head, img),
            P(img, head),
            P(head, img),
        ),
        check_vma=False,
    )
```

```python
import functools

import jax
import jax.numpy as jnp
from jax import lax
from jax.experimental import pallas as pl
from jax.experimental.pallas import tpu as pltpu
from jax.sharding import Mesh, PartitionSpec as P

SIZE = {"yl": 2, "x": 4, "z": 8, "yh": 2, "core": 2}
BF = jnp.bfloat16
F32 = jnp.float32
VM = pl.BlockSpec(memory_space=pltpu.VMEM)
SM = pl.BlockSpec(memory_space=pltpu.SMEM)
MIB = 1024 * 1024
ROOT = 0.7978845608028654


def shift(array, axis, by):
    n = SIZE[axis]
    return lax.ppermute(array, axis, [(i, (i + by) % n) for i in range(n)])


def dot(a, b, ca, cb):
    return lax.dot_general(a, b, (((ca,), (cb,)), ((), ())), preferred_element_type=F32)


def call(kernel, outs, args, scratch=(), flops=0, limit=24):
    moved = sum(a.size * a.dtype.itemsize for a in args[1:])
    moved += sum(o.size * o.dtype.itemsize for o in outs)
    return pl.pallas_call(
        kernel,
        out_shape=outs,
        in_specs=[SM] + [VM] * (len(args) - 1),
        out_specs=[VM] * len(outs),
        scratch_shapes=list(scratch),
        compiler_params=pltpu.CompilerParams(vmem_limit_bytes=limit * MIB),
        cost_estimate=pl.CostEstimate(flops=flops, bytes_accessed=moved, transcendentals=0),
    )(*args)


def sds(shape, dtype=BF):
    return jax.ShapeDtypeStruct(shape, dtype)


def norm_parts(rows):
    centre = rows - jnp.mean(rows, axis=-1, keepdims=True)
    factor = lax.rsqrt(jnp.mean(centre * centre, axis=-1, keepdims=True) + 1e-06)
    return centre * factor, factor


def back(rows, grad):
    normed, factor = norm_parts(rows)
    return factor * (
        grad
        - jnp.mean(grad, axis=-1, keepdims=True)
        - normed * jnp.mean(grad * normed, axis=-1, keepdims=True)
    )


def mlp_kernel(pos, middle, out_grad, w_up, w_down, nm, hidden, pre_grad, send, keep, acc):
    core = pos[3]
    nm[...] = norm_parts(middle[...].astype(F32))[0].astype(BF)
    width = w_up.shape[1]
    for lo in range(0, width, 256):
        cols = slice(lo, min(lo + 256, width))
        p = dot(nm[...], w_up[:, cols], 1, 0)
        hg = dot(out_grad[...], w_down[cols, :], 1, 1)
        sq = p * p
        t = jnp.tanh(ROOT * (p * (1.0 + 0.044715 * sq)))
        half = 0.5 * (1.0 + t)
        hidden[:, cols] = (p * half).astype(BF)
        slope = half + 0.5 * p * (1.0 - t * t) * (ROOT * (1.0 + 3 * 0.044715 * sq))
        pre_grad[:, cols] = (slope * hg).astype(BF)
    acc[...] = dot(pre_grad[...], w_up[...], 1, 1).reshape(acc.shape)
    for part in range(2):
        keep[part] = acc[2 * part + core]
        send[part] = acc[2 * part + 1 - core].astype(BF)


def terms_x(pos, a, b, scratch, outs):
    x = pos[1]
    half = a.shape[1] // 2
    for y in range(2):
        t = dot(a[:, y * half : (y + 1) * half], b[...], 0, 0).astype(BF)
        scratch[y] = t.reshape(scratch.shape[1:])
    for by in range(4):
        outs[by][...] = scratch[:, lax.rem(x + by, 4)]


def terms_y(pos, a, b, scratch, own, send):
    yl = pos[0]
    half = a.shape[1] // 2
    for y in range(2):
        scratch[y] = dot(a[:, y * half : (y + 1) * half], b[...], 0, 0).astype(BF)
    own[...] = scratch[yl]
    send[...] = scratch[1 - yl]


def early_kernel(pos, out_grad, hidden, nm, pre_grad, d0, d1, d2, d3, u0, u1, s_down, s_up):
    terms_x(pos, out_grad, hidden, s_down, (d0, d1, d2, d3))
    terms_y(pos, nm, pre_grad, s_up, u0, u1)


def add_one_kernel(pos, x0, x1, x2, x3, y0, y1, xkeep, xsend, k0, s1, s2, s3, s_x, s_y):
    yl, x = pos[0], pos[1]
    s_x[...] = x0[...].astype(F32) + x2[...].astype(F32) + x1[...].astype(F32) + x3[...].astype(F32)
    xkeep[...] = s_x[yl]
    xsend[...] = s_x[1 - yl].astype(BF)
    s_y[...] = (y0[...].astype(F32) + y1[...].astype(F32)).reshape(s_y.shape)
    k0[...] = s_y[x]
    for by, out in ((1, s1), (2, s2), (3, s3)):
        out[...] = s_y[lax.rem(x + by, 4)].astype(BF)


def add_two_kernel(pos, xkeep, xrecv, k0, r1, r2, r3, out):
    cols = xkeep.shape[1]
    first = (xkeep[...] + xrecv[...].astype(F32)).astype(BF)
    second = k0[...] + r2[...].astype(F32) + r1[...].astype(F32) + r3[...].astype(F32)
    second = second.astype(BF)
    for k in range(8):
        out[k, :, :cols] = first[20 * k : 20 * k + 20]
        out[k, :, cols:] = second[20 * k : 20 * k + 20]


def by_head(maps, columns, contract):
    heads = maps.shape[0]
    size = columns.shape[1] // heads
    lane = lax.broadcasted_iota(jnp.int32, columns.shape, 1)
    total = None
    for h in range(heads):
        mine = (lane >= h * size) & (lane < (h + 1) * size)
        part = jnp.where(mine, columns, jnp.zeros_like(columns)).astype(BF)
        part = dot(maps[h], part, contract, 0)
        total = part if total is None else total + part
    return total


def values_kernel(pos, inputs, w_value, maps, ni, attended):
    ni[...] = norm_parts(inputs[...].astype(F32))[0].astype(BF)
    values = dot(ni[...], w_value[...], 1, 0).astype(BF).astype(F32)
    attended[...] = by_head(maps, values, 1).astype(BF)


def core_sum_kernel(pos, keep, recv, total, total_b):
    s = keep[...] + recv[...].astype(F32)
    total[...] = s
    total_b[...] = s.astype(BF)


def mid_kernel(pos, total, recv, middle, out_grad, own, mid_b):
    yh, core = pos[2], pos[3]
    for part in range(2):
        rows = middle[2 * part + core].astype(F32)
        grad = total[part] + recv[part].astype(F32)
        mid = out_grad[2 * part + core].astype(F32) + back(rows, grad)
        mid_b[part] = mid.astype(BF)

        @pl.when(yh == part)
        def _():
            own[...] = mid


def late_kernel(
    pos, mid_b, other_b, maps, w_out, w_value, attended, ni,
    send, keep, o0, o1, o2, o3, v0, v1, mgb, acc, vg, s_out, s_val,
):
    core = pos[3]
    for part in range(2):
        mgb[2 * part + core] = mid_b[part]
        mgb[2 * part + 1 - core] = other_b[part]
    grad = mgb[...].reshape(4 * mgb.shape[1], mgb.shape[2])
    att = dot(grad, w_out[...], 1, 1).astype(BF).astype(F32)
    vg[...] = by_head(maps, att, 0).astype(BF)
    acc[...] = dot(vg[...], w_value[...], 1, 1).reshape(acc.shape)
    for part in range(2):
        keep[part] = acc[2 * part + core]
        send[part] = acc[2 * part + 1 - core].astype(BF)
    terms_x(pos, grad, attended, s_out, (o0, o1, o2, o3))
    terms_y(pos, ni, vg, s_val, v0, v1)


def in_sum_kernel(pos, keep, recv, own, send):
    yh = pos[2]
    own[...] = keep[yh] + recv[yh].astype(F32)
    send[...] = (keep[1 - yh] + recv[1 - yh].astype(F32)).astype(BF)


def in_grad_kernel(pos, own, recv, inputs, mid_own, out):
    row = 2 * pos[2] + pos[3]
    grad = own[...] + recv[...].astype(F32)
    out[...] = (mid_own[...] + back(inputs[row].astype(F32), grad)).astype(BF)


def image_sum(pos, xs, ys, cols):
    r = [shift(xs[by], "x", by) for by in (1, 2, 3)]
    yr = shift(ys[1], "yl", 1)
    xkeep, xsend, k0, s1, s2, s3 = call(
        add_one_kernel,
        [sds((160, cols), F32), sds((160, cols)), sds((160, cols), F32)] + [sds((160, cols))] * 3,
        (pos, xs[0], r[0], r[1], r[2], ys[0], yr),
        [pltpu.VMEM((2, 160, cols), F32), pltpu.VMEM((4, 160, cols), F32)],
    )
    q = [shift(s, "x", by) for s, by in ((s1, 1), (s2, 2), (s3, 3))]
    xr = shift(xsend, "yl", 1)
    (blocks,) = call(
        add_two_kernel, [sds((8, 20, 2 * cols))], (pos, xkeep, xr, k0, q[0], q[1], q[2])
    )
    parts = lax.all_to_all(blocks, "z", 0, 0)
    total = jnp.sum(parts.astype(F32), axis=0)
    return total[:, :cols].T, total[:, cols:]


def on_device(inputs, middle, out_grad, cached_maps, w_value, w_out, w_up, w_down):
    tok, d = inputs.shape
    ff, ev = w_up.shape[1], w_value.shape[1]
    share = tok // 4
    maps_here = cached_maps[0]
    pos = jnp.stack([lax.axis_index(a) for a in ("yl", "x", "yh", "core")]).astype(jnp.int32)
    rows4 = (4, share, d)
    rows2 = (2, share, d)

    nm, hidden, pre_grad, mid_send, mid_keep = call(
        mlp_kernel,
        [sds((tok, d)), sds((tok, ff)), sds((tok, ff)), sds(rows2), sds(rows2, F32)],
        (pos, middle, out_grad, w_up, w_down),
        [pltpu.VMEM(rows4, F32)],
        flops=6 * tok * d * ff,
    )
    mid_recv = shift(mid_send, "core", 1)
    early = call(
        early_kernel,
        [sds((2, 160, ff))] * 4 + [sds((640, ff))] * 2,
        (pos, out_grad, hidden, nm, pre_grad),
        [pltpu.VMEM((2, 4, 160, ff), BF), pltpu.VMEM((2, 640, ff), BF)],
        flops=4 * tok * d * ff,
    )
    mid_total, mid_total_b = call(core_sum_kernel, [sds(rows2, F32), sds(rows2)], (pos, mid_keep, mid_recv))
    mid_other = shift(mid_total_b, "yh", 1)
    ni, attended = call(
        values_kernel,
        [sds((tok, d)), sds((tok, ev))],
        (pos, inputs, w_value, maps_here),
        flops=4 * tok * d * ev,
    )
    mid_own, mid_b = call(
        mid_kernel,
        [sds((share, d), F32), sds(rows2)],
        (pos, mid_total, mid_other, middle.reshape(rows4), out_grad.reshape(rows4)),
    )
    other_b = shift(mid_b, "core", 1)
    late = call(
        late_kernel,
        [sds(rows2), sds(rows2, F32)] + [sds((2, 160, ev))] * 4 + [sds((640, ev))] * 2,
        (pos, mid_b, other_b, maps_here, w_out, w_value, attended, ni),
        [
            pltpu.VMEM(rows4, BF),
            pltpu.VMEM(rows4, F32),
            pltpu.VMEM((tok, ev), BF),
            pltpu.VMEM((2, 4, 160, ev), BF),
            pltpu.VMEM((2, 640, ev), BF),
        ],
        flops=10 * tok * d * ev,
    )
    in_recv = shift(late[0], "core", 1)
    in_own, in_send = call(in_sum_kernel, [sds((share, d), F32), sds((share, d))], (pos, late[1], in_recv))
    in_other = shift(in_send, "yh", 1)
    (in_grad,) = call(
        in_grad_kernel, [sds((share, d))], (pos, in_own, in_other, inputs.reshape(rows4), mid_own)
    )
    grad_down, grad_up = image_sum(pos, early[:4], early[4:], ff)
    grad_out, grad_value = image_sum(pos, late[2:6], late[6:], ev)
    return (in_grad, grad_value, grad_out, grad_up, grad_down)


def solution(mesh):
    split = Mesh(mesh.devices.reshape(2, 4, 8, 2, 2), ("yl", "x", "z", "yh", "core"))
    img, head = ("yl", "x", "z"), ("yh", "core")
    return jax.shard_map(
        on_device,
        mesh=split,
        in_specs=(
            P(img, None),
            P(img, None),
            P(img, None),
            P(img, head, None, None),
            P(None, head),
            P(head, None),
            P(None, head),
            P(head, None),
        ),
        out_specs=(
            P(img + head, None),
            P(img, head),
            P(head, img),
            P(img, head),
            P(head, img),
        ),
        check_vma=False,
    )
```

```python
import jax
import jax.numpy as jnp
from jax import lax
from jax.experimental import pallas as pl
from jax.experimental.pallas import tpu as pltpu
from jax.sharding import Mesh, PartitionSpec as P

SIZE = {"yl": 2, "x": 4, "yh": 2, "core": 2}
BF = jnp.bfloat16
F32 = jnp.float32
VM = pl.BlockSpec(memory_space=pltpu.VMEM)
SM = pl.BlockSpec(memory_space=pltpu.SMEM)
HB = pl.BlockSpec(memory_space=pl.ANY)
MIB = 1024 * 1024
ROOT = 0.7978845608028654


def shift(array, axis, by):
    n = SIZE[axis]
    return lax.ppermute(array, axis, [(i, (i + by) % n) for i in range(n)])


def swap_z(array, first):
    pairs = []
    for i in range(first, 8 + first, 2):
        pairs += [(i % 8, (i + 1) % 8), ((i + 1) % 8, i % 8)]
    return lax.ppermute(array, ("zh", "zl"), pairs)


def dot(a, b, ca, cb):
    return lax.dot_general(a, b, (((ca,), (cb,)), ((), ())), preferred_element_type=F32)


def call(kernel, outs, args, scratch=(), flops=0, limit=24, after=(), held=()):
    moved = sum(a.size * a.dtype.itemsize for a in args[1:])
    moved += sum(o.size * o.dtype.itemsize for o in outs)
    n, m = len(args), len(after)

    def body(*refs):
        kernel(*refs[:n], *refs[n + m :])

    specs = [SM] + [HB if i in held else VM for i in range(1, n)] + [HB] * m
    return pl.pallas_call(
        body,
        out_shape=outs,
        in_specs=specs,
        out_specs=[VM] * len(outs),
        scratch_shapes=list(scratch),
        compiler_params=pltpu.CompilerParams(vmem_limit_bytes=limit * MIB),
        cost_estimate=pl.CostEstimate(flops=flops, bytes_accessed=moved, transcendentals=0),
        name=kernel.__name__,
    )(*args, *after)


def sds(shape, dtype=BF):
    return jax.ShapeDtypeStruct(shape, dtype)


def norm_parts(rows):
    centre = rows - jnp.mean(rows, axis=-1, keepdims=True)
    factor = lax.rsqrt(jnp.mean(centre * centre, axis=-1, keepdims=True) + 1e-06)
    return centre * factor, factor


def back(rows, grad):
    normed, factor = norm_parts(rows)
    return factor * (
        grad
        - jnp.mean(grad, axis=-1, keepdims=True)
        - normed * jnp.mean(grad * normed, axis=-1, keepdims=True)
    )


def mlp_kernel(
    pos, middle_h, grad_h, up_h, down_h,
    nm, hidden, pre_grad, send, keep, middle, out_grad, w_up, w_down, acc, sems,
):
    core = pos[3]
    copies = [
        pltpu.make_async_copy(src, dst, sems.at[i])
        for i, (src, dst) in enumerate(
            ((middle_h, middle), (up_h, w_up), (grad_h, out_grad), (down_h, w_down))
        )
    ]
    for c in copies:
        c.start()
    copies[0].wait()
    nm[...] = norm_parts(middle[...].astype(F32))[0].astype(BF)
    copies[1].wait()
    copies[2].wait()
    copies[3].wait()
    width = w_up.shape[1]
    for lo in range(0, width, 256):
        cols = slice(lo, min(lo + 256, width))
        p = dot(nm[...], w_up[:, cols], 1, 0)
        hg = dot(out_grad[...], w_down[cols, :], 1, 1)
        sq = p * p
        t = jnp.tanh(ROOT * (p * (1.0 + 0.044715 * sq)))
        half = 0.5 * (1.0 + t)
        hidden[:, cols] = (p * half).astype(BF)
        slope = half + 0.5 * p * (1.0 - t * t) * (ROOT * (1.0 + 3 * 0.044715 * sq))
        pre_grad[:, cols] = (slope * hg).astype(BF)
    acc[...] = dot(pre_grad[...], w_up[...], 1, 1).reshape(acc.shape)
    for part in range(2):
        keep[part] = acc[2 * part + core]
        send[part] = acc[2 * part + 1 - core].astype(BF)


def ordering():
    new = lax.broadcasted_iota(jnp.int32, (640, 1), 0)
    parity, rest = new // 320, new % 320
    x, rest = rest // 80, rest % 80
    old = x * 160 + (2 * (rest // 20) + parity) * 20 + rest % 20
    return (lax.broadcasted_iota(jnp.int32, (640, 640), 1) == old).astype(F32).astype(BF)


def terms(a, b, order, scratch):
    for y in range(2):
        left = dot(order, a[:, 640 * y : 640 * y + 640], 1, 1).astype(BF)
        for at, part in b:
            t = dot(left, part, 1, 0).astype(BF)
            width = part.shape[1]
            scratch[y, :, :, :, at : at + width] = t.reshape(2, 4, 80, width)


def early_kernel(pos, out_grad, hidden, nm, pre_grad, d0, d1, d2, d3, keep, to_a, to_b, down, up):
    zl, x = pos[0], pos[1]
    order = ordering()
    terms(nm[...], [(0, pre_grad[...])], order, up)
    for y, out in ((0, to_a), (1, to_b)):
        keep[y] = up[y, zl]
        out[...] = up[y, 1 - zl]
    terms(out_grad[...], [(0, hidden[...])], order, down)
    for by, out in enumerate((d0, d1, d2, d3)):
        out[...] = down[:, :, lax.rem(x + by, 4)]


def z_sum(pos, keep, from_a, from_b, total, k0, sends):
    x = pos[1]
    total[0] = keep[0].astype(F32) + from_a[...].astype(F32)
    total[1] = keep[1].astype(F32) + from_b[...].astype(F32)
    k0[...] = total[:, x]
    for by, out in zip((1, 2, 3), sends):
        out[...] = total[:, lax.rem(x + by, 4)].astype(BF)


def add_early_kernel(
    pos, d0, d1, d2, d3, keep, from_a, from_b,
    dk, to_a, to_b, k0, s1, s2, s3, s_d, s_u,
):
    zl = pos[0]
    s_d[...] = d0[...].astype(F32) + d2[...].astype(F32) + d1[...].astype(F32) + d3[...].astype(F32)
    dk[...] = s_d[:, zl]
    to_a[...] = s_d[0, 1 - zl].astype(BF)
    to_b[...] = s_d[1, 1 - zl].astype(BF)
    z_sum(pos, keep, from_a, from_b, s_u, k0, (s1, s2, s3))


def add_late_kernel(pos, keep, from_a, from_b, k0, s1, s2, s3, s_u):
    z_sum(pos, keep, from_a, from_b, s_u, k0, (s1, s2, s3))


def blocks(out, total, at):
    cols = total.shape[2]
    for y in range(2):
        for k in range(4):
            out[4 * y + k, :, at : at + cols] = total[y, 20 * k : 20 * k + 20].astype(BF)


def x_total(k0, r1, r2, r3):
    return k0[...] + r2[...].astype(F32) + r1[...].astype(F32) + r3[...].astype(F32)


def two_early_kernel(pos, dk, from_a, from_b, k0, r1, r2, r3, out, s):
    s[0] = dk[0] + from_a[...].astype(F32)
    s[1] = dk[1] + from_b[...].astype(F32)
    blocks(out, s, 0)
    s[...] = x_total(k0, r1, r2, r3)
    blocks(out, s, s.shape[2])


def two_late_kernel(pos, k0, r1, r2, r3, out, s):
    s[...] = x_total(k0, r1, r2, r3)
    blocks(out, s, 0)


def last_kernel(pos, parts, first, second):
    total = parts[0].astype(F32)
    for k in range(1, 8):
        total = total + parts[k].astype(F32)
    cols = first.shape[1]
    first[...] = total[:, :cols]
    second[...] = total[:, cols:]


def by_head(maps, columns, contract):
    heads = maps.shape[0]
    size = columns.shape[1] // heads
    lane = lax.broadcasted_iota(jnp.int32, columns.shape, 1)
    total = None
    for h in range(heads):
        mine = (lane >= h * size) & (lane < (h + 1) * size)
        part = jnp.where(mine, columns, jnp.zeros_like(columns)).astype(BF)
        part = dot(maps[h], part, contract, 0)
        total = part if total is None else total + part
    return total


def values_kernel(pos, inputs, w_value_t, maps, ni, attended):
    ni[...] = norm_parts(inputs[...].astype(F32))[0].astype(BF)
    values = dot(ni[...], w_value_t[...], 1, 1).astype(BF).astype(F32)
    attended[...] = by_head(maps, values, 1).astype(BF)


def core_sum_kernel(pos, keep, recv, total, total_b):
    s = keep[...] + recv[...].astype(F32)
    total[...] = s
    total_b[...] = s.astype(BF)


def mid_kernel(pos, total, recv, middle, out_grad, own, mid_b):
    yh, core = pos[2], pos[3]
    for part in range(2):
        rows = middle[2 * part + core].astype(F32)
        grad = total[part] + recv[part].astype(F32)
        mid = out_grad[2 * part + core].astype(F32) + back(rows, grad)
        mid_b[part] = mid.astype(BF)

        @pl.when(yh == part)
        def _():
            own[...] = mid


def late_kernel(
    pos, mid_b, other_b, maps, w_out, w_value_t, attended, ni,
    send, keep, l_keep, to_a, to_b, mgb, acc, vg, both,
):
    zl, core = pos[0], pos[3]
    for part in range(2):
        mgb[2 * part + core] = mid_b[part]
        mgb[2 * part + 1 - core] = other_b[part]
    grad = mgb[...].reshape(4 * mgb.shape[1], mgb.shape[2])
    att = dot(grad, w_out[...], 1, 1).astype(BF).astype(F32)
    vg[...] = by_head(maps, att, 0).astype(BF)
    acc[...] = dot(vg[...], w_value_t[...], 1, 0).reshape(acc.shape)
    for part in range(2):
        keep[part] = acc[2 * part + core]
        send[part] = acc[2 * part + 1 - core].astype(BF)
    order = ordering()
    cols = vg.shape[1]
    terms(grad, [(0, attended[...])], order, both)
    terms(ni[...], [(cols, vg[...])], order, both)
    for y, out in ((0, to_a), (1, to_b)):
        l_keep[y] = both[y, zl]
        out[...] = both[y, 1 - zl]


def in_sum_kernel(pos, keep, recv, own, send):
    yh = pos[2]
    own[...] = keep[yh] + recv[yh].astype(F32)
    send[...] = (keep[1 - yh] + recv[1 - yh].astype(F32)).astype(BF)


def in_grad_kernel(pos, own, recv, inputs, mid_own, out):
    row = 2 * pos[2] + pos[3]
    grad = own[...] + recv[...].astype(F32)
    out[...] = (mid_own[...] + back(inputs[row].astype(F32), grad)).astype(BF)


def on_device(inputs, middle, out_grad, cached_maps, w_value, w_out, w_up, w_down):
    tok, d = inputs.shape
    ff, ev = w_up.shape[1], w_value.shape[1]
    share = tok // 4
    maps_here = cached_maps[0]
    w_value_t = w_value.T
    pos = jnp.stack([lax.axis_index(a) for a in ("zl", "x", "yh", "core")]).astype(jnp.int32)
    rows4 = (4, share, d)
    rows2 = (2, share, d)
    whole = (2, 2, 4, 80, ff)
    slab = (2, 80, ff)

    nm, hidden, pre_grad, mid_send, mid_keep = call(
        mlp_kernel,
        [sds((tok, d)), sds((tok, ff)), sds((tok, ff)), sds(rows2), sds(rows2, F32)],
        (pos, middle, out_grad, w_up, w_down),
        [
            pltpu.VMEM((tok, d), BF),
            pltpu.VMEM((tok, d), BF),
            pltpu.VMEM((d, ff), BF),
            pltpu.VMEM((ff, d), BF),
            pltpu.VMEM(rows4, F32),
            pltpu.SemaphoreType.DMA((4,)),
        ],
        flops=6 * tok * d * ff,
        limit=56,
        held=(1, 2, 3, 4),
    )
    mid_recv = shift(mid_send, "core", 1)
    ni, attended = call(
        values_kernel,
        [sds((tok, d)), sds((tok, ev))],
        (pos, inputs, w_value_t, maps_here),
        flops=4 * tok * d * ev,
        after=(mid_send,),
    )
    mid_total, mid_total_b = call(
        core_sum_kernel, [sds(rows2, F32), sds(rows2)], (pos, mid_keep, mid_recv), after=(attended,)
    )
    mid_other = shift(mid_total_b, "yh", 1)
    *downs, up_keep, up_a, up_b = call(
        early_kernel,
        [sds((2, 2, 80, ff))] * 4 + [sds((2, 4, 80, ff))] + [sds((4, 80, ff))] * 2,
        (pos, out_grad, hidden, nm, pre_grad),
        [pltpu.VMEM(whole, BF), pltpu.VMEM(whole, BF)],
        flops=6 * tok * d * ff,
        after=(mid_total_b,),
    )
    up_ra, up_rb = swap_z(up_a, 0), swap_z(up_b, 1)
    down_r = [shift(downs[by], "x", by) for by in (1, 2, 3)]
    mid_own, mid_b = call(
        mid_kernel,
        [sds((share, d), F32), sds(rows2)],
        (pos, mid_total, mid_other, middle.reshape(rows4), out_grad.reshape(rows4)),
        after=(up_keep,),
    )
    other_b = shift(mid_b, "core", 1)
    in_send, in_keep, late_keep, late_a, late_b = call(
        late_kernel,
        [sds(rows2), sds(rows2, F32), sds((2, 4, 80, ff))] + [sds((4, 80, ff))] * 2,
        (pos, mid_b, other_b, maps_here, w_out, w_value_t, attended, ni),
        [
            pltpu.VMEM(rows4, BF),
            pltpu.VMEM(rows4, F32),
            pltpu.VMEM((tok, ev), BF),
            pltpu.VMEM(whole, BF),
        ],
        flops=14 * tok * d * ev,
    )
    late_ra, late_rb = swap_z(late_a, 0), swap_z(late_b, 1)
    in_recv = shift(in_send, "core", 1)
    in_own, in_half = call(in_sum_kernel, [sds((share, d), F32), sds((share, d))], (pos, in_keep, in_recv))
    in_other = shift(in_half, "yh", 1)

    sends = [sds(slab)] * 3
    down_keep, down_a, down_b, up_0, *up_s = call(
        add_early_kernel,
        [sds(slab, F32), sds((80, ff)), sds((80, ff)), sds(slab, F32)] + sends,
        (pos, downs[0], *down_r, up_keep, up_ra, up_rb),
        [pltpu.VMEM((2, 2, 80, ff), F32), pltpu.VMEM((2, 4, 80, ff), F32)],
        after=(in_half,),
    )
    up_r = [shift(s, "x", by) for s, by in zip(up_s, (1, 2, 3))]
    down_ra, down_rb = swap_z(down_a, 0), swap_z(down_b, 1)
    late_0, *late_s = call(
        add_late_kernel,
        [sds(slab, F32)] + sends,
        (pos, late_keep, late_ra, late_rb),
        [pltpu.VMEM((2, 4, 80, ff), F32)],
        after=(up_0,),
    )
    late_r = [shift(s, "x", by) for s, by in zip(late_s, (1, 2, 3))]
    (early_blocks,) = call(
        two_early_kernel,
        [sds((8, 20, 2 * ff))],
        (pos, down_keep, down_ra, down_rb, up_0, *up_r),
        [pltpu.VMEM(slab, F32)],
        after=(late_0,),
    )
    early_parts = lax.all_to_all(early_blocks, ("yl", "zh"), 0, 0)
    (in_grad,) = call(
        in_grad_kernel,
        [sds((share, d))],
        (pos, in_own, in_other, inputs.reshape(rows4), mid_own),
        after=(early_blocks,),
    )
    (late_blocks,) = call(
        two_late_kernel,
        [sds((8, 20, ff))],
        (pos, late_0, *late_r),
        [pltpu.VMEM(slab, F32)],
        after=(in_grad,),
    )
    late_parts = lax.all_to_all(late_blocks, ("yl", "zh"), 0, 0)
    grad_down, grad_up = call(last_kernel, [sds((20, ff), F32)] * 2, (pos, early_parts), after=(late_blocks,))
    grad_out, grad_value = call(last_kernel, [sds((20, ev), F32)] * 2, (pos, late_parts), after=(grad_up,))
    return (in_grad, grad_value, grad_out.T, grad_up, grad_down.T)


def solution(mesh):
    split = Mesh(mesh.devices.reshape(2, 4, 4, 2, 2, 2), ("yl", "x", "zh", "zl", "yh", "core"))
    img, head = ("yl", "x", "zh", "zl"), ("yh", "core")
    return jax.shard_map(
        on_device,
        mesh=split,
        in_specs=(
            P(img, None),
            P(img, None),
            P(img, None),
            P(img, head, None, None),
            P(None, head),
            P(head, None),
            P(None, head),
            P(head, None),
        ),
        out_specs=(
            P(img + head, None),
            P(img, head),
            P(head, img),
            P(img, head),
            P(head, img),
        ),
        check_vma=False,
    )
```

```python
import jax
import jax.numpy as jnp
from jax import lax
from jax.experimental import pallas as pl
from jax.experimental.pallas import tpu as pltpu
from jax.sharding import Mesh, PartitionSpec as P

SIZE = {"yl": 2, "x": 4, "yh": 2, "core": 2}
BF = jnp.bfloat16
F32 = jnp.float32
VM = pl.BlockSpec(memory_space=pltpu.VMEM)
HB = pl.BlockSpec(memory_space=pl.ANY)
MIB = 1024 * 1024
ROOT = 0.7978845608028654
WORK = dict(
    mlp=3e9, early=4e8, core_sum=0, values=1e9, mid=3e9, late=8e8, in_part=4e8, in_sum=0, add_early=2e8,
    add_late=0, in_grad=2e8, two_early=2e8, two_late=1e10, last_early=1e9,
    last_late=0,
)


def shift(array, axis, by):
    n = SIZE[axis]
    return lax.ppermute(array, axis, [(i, (i + by) % n) for i in range(n)])


def swap_z(array, first):
    pairs = []
    for i in range(first, 8 + first, 2):
        pairs += [(i % 8, (i + 1) % 8), ((i + 1) % 8, i % 8)]
    return lax.ppermute(array, ("zh", "zl"), pairs)


def shift_yz(array, y, z):
    pairs = [(4 * i + k, 4 * ((i + y) % 2) + (k + z) % 4) for i in range(2) for k in range(4)]
    return lax.ppermute(array, ("yl", "zh"), pairs)


def dot(a, b, ca, cb):
    return lax.dot_general(a, b, (((ca,), (cb,)), ((), ())), preferred_element_type=F32)


def call(kernel, outs, args, scratch=(), limit=24, after=None):
    n = len(args)
    moved = sum(a.size * a.dtype.itemsize for a in args)
    moved += sum(o.size * o.dtype.itemsize for o in outs)
    tokens = [] if after is None else [after]

    def body(*refs):
        refs = list(refs)
        refs.pop(n + len(tokens) + len(outs))
        pos = [lax.axis_index(a) for a in ("zl", "x", "yh", "core", "yl", "zh")]
        kernel(pos, *refs[:n], *refs[n + len(tokens) :])

    return pl.pallas_call(
        body,
        out_shape=list(outs) + [sds((8, 128), F32)],
        in_specs=[VM] * n + [HB] * len(tokens),
        out_specs=[VM] * len(outs) + [HB],
        scratch_shapes=list(scratch),
        compiler_params=pltpu.CompilerParams(vmem_limit_bytes=limit * MIB),
        cost_estimate=pl.CostEstimate(flops=int(WORK[kernel.__name__.removesuffix('_kernel')]), bytes_accessed=moved, transcendentals=0),
        name=kernel.__name__,
    )(*args, *tokens)


def sds(shape, dtype=BF):
    return jax.ShapeDtypeStruct(shape, dtype)


def norm_parts(rows):
    centre = rows - jnp.mean(rows, axis=-1, keepdims=True)
    factor = lax.rsqrt(jnp.mean(centre * centre, axis=-1, keepdims=True) + 1e-06)
    return centre * factor, factor


def back(rows, grad):
    normed, factor = norm_parts(rows)
    return factor * (
        grad
        - jnp.mean(grad, axis=-1, keepdims=True)
        - normed * jnp.mean(grad * normed, axis=-1, keepdims=True)
    )


def mlp_kernel(pos, middle, out_grad, w_up, w_down, nm, hidden, pre_grad, send, keep, acc):
    core = pos[3]
    width = w_up.shape[1]
    nm[...] = norm_parts(middle[...].astype(F32))[0].astype(BF)
    for lo in range(0, width, 256):
        cols = slice(lo, min(lo + 256, width))
        p = dot(nm[...], w_up[:, cols], 1, 0)
        hg = dot(out_grad[...], w_down[cols, :], 1, 1)
        sq = p * p
        t = jnp.tanh(ROOT * (p * (1.0 + 0.044715 * sq)))
        half = 0.5 * (1.0 + t)
        hidden[:, cols] = (p * half).astype(BF)
        slope = half + 0.5 * p * (1.0 - t * t) * (ROOT * (1.0 + 3 * 0.044715 * sq))
        pre_grad[:, cols] = (slope * hg).astype(BF)
    acc[...] = dot(pre_grad[...], w_up[...], 1, 1).reshape(acc.shape)
    for part in range(2):
        keep[part] = acc[2 * part + core]
        send[part] = acc[2 * part + 1 - core].astype(BF)


def ordering(pos):
    zl, x = pos[0], pos[1]
    new = lax.broadcasted_iota(jnp.int32, (640, 1), 0)
    other, rest = new // 320, new % 320
    parity = zl + other - 2 * zl * other
    by, rest = rest // 80, rest % 80
    z = 2 * (rest // 20) + parity
    old = (x + by) % 4 * 160 + z * 20 + rest % 20
    return (lax.broadcasted_iota(jnp.int32, (640, 640), 1) == old).astype(F32).astype(BF)


def turned(pos, order, a, y):
    at = pl.multiple_of((pos[4] + y - 2 * pos[4] * y) * 640, 640)
    return dot(order[...], a[:, pl.ds(at, 640)], 1, 1).astype(BF)


def put(keep, to, y, at, left, b):
    cols = b.shape[1]
    t = dot(left, b[...], 1, 0).astype(BF).reshape(2, 4, 80, cols)
    keep[y, :, :, at : at + cols] = t[0]
    to[:, :, at : at + cols] = t[1]


def early_kernel(pos, out_grad, hidden, nm, pre_grad, keep, to_a, to_b, order):
    order[...] = ordering(pos)
    cols = hidden.shape[1]
    for y, out in ((0, to_a), (1, to_b)):
        put(keep, out, y, 0, turned(pos, order, out_grad, y), hidden)
        put(keep, out, y, cols, turned(pos, order, nm, y), pre_grad)


def z_sum(pos, keep, from_a, from_b, k0, s1, s2, s3):
    for y, recv in ((0, from_a), (1, from_b)):
        for by, out in enumerate((k0, s1, s2, s3)):
            total = keep[y, by].astype(F32) + recv[by].astype(F32)
            out[y] = total.astype(out.dtype)


def add_early_kernel(*refs):
    z_sum(*refs)


def add_late_kernel(*refs):
    z_sum(*refs)


def x_sum(k0, r1, r2, r3, s):
    s[...] = k0[...] + r2[...].astype(F32) + r1[...].astype(F32) + r3[...].astype(F32)


def two_early_kernel(pos, k0, r1, r2, r3, out, s):
    x_sum(k0, r1, r2, r3, s)
    yl = pos[4]
    for y in range(2):
        for k in range(4):
            out[4 * (yl + y - 2 * yl * y) + k] = s[y, 20 * k : 20 * k + 20].astype(BF)


def two_late_kernel(pos, k0, r1, r2, r3, *rest):
    *outs, s, cut = rest
    x_sum(k0, r1, r2, r3, s)
    for y in range(2):
        for k in range(4):
            cut[y, k] = s[y, 20 * k : 20 * k + 20]
    for i, out in enumerate(outs):
        out[...] = cut[i // 4, lax.rem(pos[5] + i % 4, 4)].astype(out.dtype)


def last_early_kernel(pos, parts, first, second):
    total = parts[0].astype(F32)
    for k in range(1, 8):
        total = total + parts[k].astype(F32)
    cols = first.shape[1]
    first[...] = total[:, :cols]
    second[...] = total[:, cols:]


def last_late_kernel(pos, own, *rest):
    *parts, first, second = rest
    total = own[...]
    for part in parts:
        total = total + part[...].astype(F32)
    cols = first.shape[1]
    first[...] = total[:, :cols]
    second[...] = total[:, cols:]


def by_head(maps, columns, contract):
    heads = maps.shape[0]
    size = columns.shape[1] // heads
    lane = lax.broadcasted_iota(jnp.int32, columns.shape, 1)
    total = None
    for h in range(heads):
        mine = (lane >= h * size) & (lane < (h + 1) * size)
        part = jnp.where(mine, columns, jnp.zeros_like(columns)).astype(BF)
        part = dot(maps[h], part, contract, 0)
        total = part if total is None else total + part
    return total


def values_kernel(pos, inputs, w_value_t, maps, order, ni_turned, attended, ni):
    ni[...] = norm_parts(inputs[...].astype(F32))[0].astype(BF)
    values = dot(ni[...], w_value_t[...], 1, 1).astype(BF).astype(F32)
    attended[...] = by_head(maps, values, 1).astype(BF)
    for y in range(2):
        ni_turned[y] = turned(pos, order, ni, y)


def core_sum_kernel(pos, keep, recv, total, total_b):
    s = keep[...] + recv[...].astype(F32)
    total[...] = s
    total_b[...] = s.astype(BF)


def mid_kernel(pos, total, recv, middle, out_grad, own, mid_b):
    yh, core = pos[2], pos[3]
    for part in range(2):
        rows = middle[2 * part + core].astype(F32)
        grad = total[part] + recv[part].astype(F32)
        mid = out_grad[2 * part + core].astype(F32) + back(rows, grad)
        mid_b[part] = mid.astype(BF)

        @pl.when(yh == part)
        def _():
            own[...] = mid


def late_kernel(
    pos, mid_b, other_b, maps, w_out, attended, ni_turned, order, vg, keep, to_a, to_b, mgb
):
    core = pos[3]
    share = mid_b.shape[1]
    for part in range(2):
        for c, rows in ((core, mid_b), (1 - core, other_b)):
            mgb[pl.ds(pl.multiple_of((2 * part + c) * share, share), share)] = rows[part]
    att = dot(mgb[...], w_out[...], 1, 1).astype(BF).astype(F32)
    vg[...] = by_head(maps, att, 0).astype(BF)
    cols = vg.shape[1]
    for y, out in ((0, to_a), (1, to_b)):
        put(keep, out, y, 0, turned(pos, order, mgb, y), attended)
        put(keep, out, y, cols, ni_turned[y], vg)


def in_part_kernel(pos, vg, w_value_t, send, keep, acc):
    core = pos[3]
    acc[...] = dot(vg[...], w_value_t[...], 1, 0).reshape(acc.shape)
    for part in range(2):
        keep[part] = acc[2 * part + core]
        send[part] = acc[2 * part + 1 - core].astype(BF)


def in_sum_kernel(pos, keep, recv, own, send):
    yh = pos[2]
    own[...] = keep[yh] + recv[yh].astype(F32)
    send[...] = (keep[1 - yh] + recv[1 - yh].astype(F32)).astype(BF)


def in_grad_kernel(pos, own, recv, inputs, mid_own, out):
    row = 2 * pos[2] + pos[3]
    grad = own[...] + recv[...].astype(F32)
    out[...] = (mid_own[...] + back(inputs[row].astype(F32), grad)).astype(BF)


def on_device(inputs, middle, out_grad, cached_maps, w_value, w_out, w_up, w_down):
    tok, d = inputs.shape
    ff, ev = w_up.shape[1], w_value.shape[1]
    share = tok // 4
    maps_here = cached_maps[0]
    w_value_t = w_value.T
    rows4 = (4, share, d)
    rows2 = (2, share, d)
    half = (4, 80, ff)
    slab = (2, 80, ff)

    nm, hidden, pre_grad, mid_send, mid_keep, t = call(
        mlp_kernel,
        [sds((tok, d)), sds((tok, ff)), sds((tok, ff)), sds(rows2), sds(rows2, F32)],
        (middle, out_grad, w_up, w_down),
        [pltpu.VMEM(rows4, F32)],
    )
    mid_recv = shift(mid_send, "core", 1)

    def image_terms(cols):
        return [sds((2, 4, 80, cols)), sds((4, 80, cols)), sds((4, 80, cols))]

    early_keep, early_a, early_b, order, t = call(
        early_kernel,
        image_terms(2 * ff) + [sds((640, 640))],
        (out_grad, hidden, nm, pre_grad),
        after=t,
    )
    early_ra, early_rb = swap_z(early_a, 0), swap_z(early_b, 1)
    mid_total, mid_total_b, t = call(
        core_sum_kernel, [sds(rows2, F32), sds(rows2)], (mid_keep, mid_recv), after=t
    )
    mid_other = shift(mid_total_b, "yh", 1)
    ni_turned, attended, t = call(
        values_kernel,
        [sds((2, 640, tok)), sds((tok, ev))],
        (inputs, w_value_t, maps_here, order),
        [pltpu.VMEM((tok, d), BF)],
        after=t,
    )
    mid_own, mid_b, t = call(
        mid_kernel,
        [sds((share, d), F32), sds(rows2)],
        (mid_total, mid_other, middle.reshape(rows4), out_grad.reshape(rows4)),
        after=t,
    )
    other_b = shift(mid_b, "core", 1)
    vg, late_keep, late_a, late_b, t = call(
        late_kernel,
        [sds((tok, ev))] + image_terms(2 * ev),
        (mid_b, other_b, maps_here, w_out, attended, ni_turned, order),
        [pltpu.VMEM((tok, d), BF)],
        after=t,
    )
    late_ra, late_rb = swap_z(late_a, 0), swap_z(late_b, 1)
    def add(kernel, args, cols, after):
        k0, s1, s2, s3, after = call(
            kernel, [sds((2, 80, cols), F32)] + [sds((2, 80, cols))] * 3, args, after=after
        )
        return [k0] + [shift(s, "x", by) for s, by in ((s1, 1), (s2, 2), (s3, 3))], after

    in_send, in_keep, t = call(
        in_part_kernel, [sds(rows2), sds(rows2, F32)], (vg, w_value_t), [pltpu.VMEM(rows4, F32)], after=t
    )
    in_recv = shift(in_send, "core", 1)
    in_own, in_half, t = call(
        in_sum_kernel, [sds((share, d), F32), sds((share, d))], (in_keep, in_recv), after=t
    )
    in_other = shift(in_half, "yh", 1)
    early_x, t = add(add_early_kernel, (early_keep, early_ra, early_rb), 2 * ff, t)
    late_x, t = add(add_late_kernel, (late_keep, late_ra, late_rb), 2 * ev, t)
    in_grad, t = call(
        in_grad_kernel,
        [sds((share, d))],
        (in_own, in_other, inputs.reshape(rows4), mid_own),
        after=t,
    )
    early_blocks, t = call(
        two_early_kernel,
        [sds((8, 20, 2 * ff))],
        early_x,
        [pltpu.VMEM((2, 80, 2 * ff), F32)],
        after=t,
    )
    early_parts = lax.all_to_all(early_blocks, ("yl", "zh"), 0, 0)
    late_own, *late_s, t = call(
        two_late_kernel,
        [sds((20, 2 * ev), F32)] + [sds((20, 2 * ev))] * 7,
        late_x,
        [pltpu.VMEM((2, 80, 2 * ev), F32), pltpu.VMEM((2, 4, 20, 2 * ev), F32)],
        after=t,
    )
    late_r = [shift_yz(block, i // 4, i % 4) for i, block in enumerate(late_s, 1)]
    grad_down, grad_up, t = call(last_early_kernel, [sds((20, ff), F32)] * 2, (early_parts,), after=t)
    grad_out, grad_value, t = call(
        last_late_kernel, [sds((20, ev), F32)] * 2, (late_own, *late_r), after=t
    )
    return (in_grad, grad_value, grad_out.T, grad_up, grad_down.T)


def solution(mesh):
    split = Mesh(mesh.devices.reshape(2, 4, 4, 2, 2, 2), ("yl", "x", "zh", "zl", "yh", "core"))
    img, head = ("yl", "x", "zh", "zl"), ("yh", "core")
    return jax.shard_map(
        on_device,
        mesh=split,
        in_specs=(
            P(img, None),
            P(img, None),
            P(img, None),
            P(img, head, None, None),
            P(None, head),
            P(head, None),
            P(None, head),
            P(head, None),
        ),
        out_specs=(
            P(img + head, None),
            P(img, head),
            P(head, img),
            P(img, head),
            P(head, img),
        ),
        check_vma=False,
    )
```

```python
import jax
import jax.numpy as jnp
from jax import lax
from jax.experimental import pallas as pl
from jax.experimental.pallas import tpu as pltpu
from jax.sharding import Mesh, PartitionSpec as P

SIZE = {"yl": 2, "x": 4, "zh": 4, "yh": 2, "core": 2}
BF = jnp.bfloat16
F32 = jnp.float32
VM = pl.BlockSpec(memory_space=pltpu.VMEM)
HB = pl.BlockSpec(memory_space=pl.ANY)
MIB = 1024 * 1024
ROOT = 0.7978845608028654
WORK = dict(
    mlp=3e9, early=4e8, core_sum=0, values=1e9, mid=3e9, late=8e8, in_part=4e8, in_sum=0, add_early=2e8,
    add_late=0, in_grad=2e8, y_early=0, two_late=2e8, two_early=2e8, two=1e10, last=0,
)


def shift(array, axis, by):
    n = SIZE[axis]
    return lax.ppermute(array, axis, [(i, (i + by) % n) for i in range(n)])


def swap_z(array, first):
    pairs = []
    for i in range(first, 8 + first, 2):
        pairs += [(i % 8, (i + 1) % 8), ((i + 1) % 8, i % 8)]
    return lax.ppermute(array, ("zh", "zl"), pairs)


def dot(a, b, ca, cb):
    return lax.dot_general(a, b, (((ca,), (cb,)), ((), ())), preferred_element_type=F32)


def call(kernel, outs, args, scratch=(), limit=24, after=None):
    n = len(args)
    moved = sum(a.size * a.dtype.itemsize for a in args)
    moved += sum(o.size * o.dtype.itemsize for o in outs)
    tokens = [] if after is None else [after]

    def body(*refs):
        refs = list(refs)
        refs.pop(n + len(tokens) + len(outs))
        pos = [lax.axis_index(a) for a in ("zl", "x", "yh", "core", "yl", "zh")]
        kernel(pos, *refs[:n], *refs[n + len(tokens) :])

    return pl.pallas_call(
        body,
        out_shape=list(outs) + [sds((8, 128), F32)],
        in_specs=[VM] * n + [HB] * len(tokens),
        out_specs=[VM] * len(outs) + [HB],
        scratch_shapes=list(scratch),
        compiler_params=pltpu.CompilerParams(vmem_limit_bytes=limit * MIB),
        cost_estimate=pl.CostEstimate(flops=int(WORK[kernel.__name__.removesuffix('_kernel')]), bytes_accessed=moved, transcendentals=0),
        name=kernel.__name__,
    )(*args, *tokens)


def sds(shape, dtype=BF):
    return jax.ShapeDtypeStruct(shape, dtype)


def norm_parts(rows):
    centre = rows - jnp.mean(rows, axis=-1, keepdims=True)
    factor = lax.rsqrt(jnp.mean(centre * centre, axis=-1, keepdims=True) + 1e-06)
    return centre * factor, factor


def back(rows, grad):
    normed, factor = norm_parts(rows)
    return factor * (
        grad
        - jnp.mean(grad, axis=-1, keepdims=True)
        - normed * jnp.mean(grad * normed, axis=-1, keepdims=True)
    )


def mlp_kernel(pos, middle, out_grad, w_up, w_down, nm, hidden, pre_grad, send, keep, acc):
    core = pos[3]
    width = w_up.shape[1]
    nm[...] = norm_parts(middle[...].astype(F32))[0].astype(BF)
    for lo in range(0, width, 256):
        cols = slice(lo, min(lo + 256, width))
        p = dot(nm[...], w_up[:, cols], 1, 0)
        hg = dot(out_grad[...], w_down[cols, :], 1, 1)
        sq = p * p
        t = jnp.tanh(ROOT * (p * (1.0 + 0.044715 * sq)))
        half = 0.5 * (1.0 + t)
        hidden[:, cols] = (p * half).astype(BF)
        slope = half + 0.5 * p * (1.0 - t * t) * (ROOT * (1.0 + 3 * 0.044715 * sq))
        pre_grad[:, cols] = (slope * hg).astype(BF)
    acc[...] = dot(pre_grad[...], w_up[...], 1, 1).reshape(acc.shape)
    for part in range(2):
        keep[part] = acc[2 * part + core]
        send[part] = acc[2 * part + 1 - core].astype(BF)


def ordering(pos):
    zl, x = pos[0], pos[1]
    new = lax.broadcasted_iota(jnp.int32, (640, 1), 0)
    other, rest = new // 320, new % 320
    parity = zl + other - 2 * zl * other
    by, rest = rest // 80, rest % 80
    z = 2 * (rest // 20) + parity
    old = (x + by) % 4 * 160 + z * 20 + rest % 20
    return (lax.broadcasted_iota(jnp.int32, (640, 640), 1) == old).astype(F32).astype(BF)


def turned(pos, order, a, y):
    at = pl.multiple_of((pos[4] + y - 2 * pos[4] * y) * 640, 640)
    return dot(order[...], a[:, pl.ds(at, 640)], 1, 1).astype(BF)


def put(keep, to, y, at, left, b):
    cols = b.shape[1]
    t = dot(left, b[...], 1, 0).astype(BF).reshape(2, 4, 80, cols)
    keep[y, :, :, at : at + cols] = t[0]
    to[:, :, at : at + cols] = t[1]


def early_kernel(pos, out_grad, hidden, nm, pre_grad, keep, to_a, to_b, order):
    order[...] = ordering(pos)
    cols = hidden.shape[1]
    for y, out in ((0, to_a), (1, to_b)):
        put(keep, out, y, 0, turned(pos, order, out_grad, y), hidden)
        put(keep, out, y, cols, turned(pos, order, nm, y), pre_grad)


def add_early_kernel(pos, keep, from_a, from_b, own, send):
    own[...] = keep[0].astype(F32) + from_a[...].astype(F32)
    send[...] = (keep[1].astype(F32) + from_b[...].astype(F32)).astype(BF)


def y_early_kernel(pos, own, recv, k0, s1, s2, s3):
    for by, out in enumerate((k0, s1, s2, s3)):
        out[...] = (own[by] + recv[by].astype(F32)).astype(out.dtype)


def add_late_kernel(pos, keep, from_a, from_b, k0, s1, s2, s3):
    for y, recv in ((0, from_a), (1, from_b)):
        for by, out in enumerate((k0, s1, s2, s3)):
            total = keep[y, by].astype(F32) + recv[by].astype(F32)
            out[y] = total.astype(out.dtype)


def x_sum(k0, r1, r2, r3):
    return k0[...] + r2[...].astype(F32) + r1[...].astype(F32) + r3[...].astype(F32)


def two_late_kernel(pos, k0, r1, r2, r3, own, send):
    total = x_sum(k0, r1, r2, r3)
    own[...] = total[0]
    send[...] = total[1].astype(BF)


def two_early_kernel(pos, k0, r1, r2, r3, total):
    total[...] = x_sum(k0, r1, r2, r3)


def two_kernel(pos, early, late, recv, *rest):
    *outs, both, cut = rest
    both[...] = late[...] + recv[...].astype(F32)
    cols = early.shape[1]
    for k in range(4):
        cut[k, :, :cols] = early[20 * k : 20 * k + 20]
        cut[k, :, cols:] = both[20 * k : 20 * k + 20]
    for i, out in enumerate(outs):
        out[...] = cut[lax.rem(pos[5] + i, 4)].astype(out.dtype)


def last_kernel(pos, own, *rest):
    parts, outs = rest[:3], rest[3:]
    total = own[...]
    for part in parts:
        total = total + part[...].astype(F32)
    at = 0
    for out in outs:
        cols = out.shape[1]
        out[...] = total[:, at : at + cols]
        at += cols


def by_head(maps, columns, contract):
    heads = maps.shape[0]
    size = columns.shape[1] // heads
    lane = lax.broadcasted_iota(jnp.int32, columns.shape, 1)
    total = None
    for h in range(heads):
        mine = (lane >= h * size) & (lane < (h + 1) * size)
        part = jnp.where(mine, columns, jnp.zeros_like(columns)).astype(BF)
        part = dot(maps[h], part, contract, 0)
        total = part if total is None else total + part
    return total


def values_kernel(pos, inputs, w_value_t, maps, order, ni_turned, attended, ni):
    ni[...] = norm_parts(inputs[...].astype(F32))[0].astype(BF)
    values = dot(ni[...], w_value_t[...], 1, 1).astype(BF).astype(F32)
    attended[...] = by_head(maps, values, 1).astype(BF)
    for y in range(2):
        ni_turned[y] = turned(pos, order, ni, y)


def core_sum_kernel(pos, keep, recv, total, total_b):
    s = keep[...] + recv[...].astype(F32)
    total[...] = s
    total_b[...] = s.astype(BF)


def mid_kernel(pos, total, recv, middle, out_grad, own, mid_b):
    yh, core = pos[2], pos[3]
    for part in range(2):
        rows = middle[2 * part + core].astype(F32)
        grad = total[part] + recv[part].astype(F32)
        mid = out_grad[2 * part + core].astype(F32) + back(rows, grad)
        mid_b[part] = mid.astype(BF)

        @pl.when(yh == part)
        def _():
            own[...] = mid


def late_kernel(
    pos, mid_b, other_b, maps, w_out, attended, ni_turned, order, vg, keep, to_a, to_b, mgb
):
    core = pos[3]
    share = mid_b.shape[1]
    for part in range(2):
        for c, rows in ((core, mid_b), (1 - core, other_b)):
            mgb[pl.ds(pl.multiple_of((2 * part + c) * share, share), share)] = rows[part]
    att = dot(mgb[...], w_out[...], 1, 1).astype(BF).astype(F32)
    vg[...] = by_head(maps, att, 0).astype(BF)
    cols = vg.shape[1]
    for y, out in ((0, to_a), (1, to_b)):
        put(keep, out, y, 0, turned(pos, order, mgb, y), attended)
        put(keep, out, y, cols, ni_turned[y], vg)


def in_part_kernel(pos, vg, w_value_t, send, keep, acc):
    core = pos[3]
    acc[...] = dot(vg[...], w_value_t[...], 1, 0).reshape(acc.shape)
    for part in range(2):
        keep[part] = acc[2 * part + core]
        send[part] = acc[2 * part + 1 - core].astype(BF)


def in_sum_kernel(pos, keep, recv, own, send):
    yh = pos[2]
    own[...] = keep[yh] + recv[yh].astype(F32)
    send[...] = (keep[1 - yh] + recv[1 - yh].astype(F32)).astype(BF)


def in_grad_kernel(pos, own, recv, inputs, mid_own, out):
    row = 2 * pos[2] + pos[3]
    grad = own[...] + recv[...].astype(F32)
    out[...] = (mid_own[...] + back(inputs[row].astype(F32), grad)).astype(BF)


def on_device(inputs, middle, out_grad, cached_maps, w_value, w_out, w_up, w_down):
    tok, d = inputs.shape
    ff, ev = w_up.shape[1], w_value.shape[1]
    share = tok // 4
    maps_here = cached_maps[0]
    w_value_t = w_value.T
    rows4 = (4, share, d)
    rows2 = (2, share, d)
    half = (4, 80, ff)
    slab = (2, 80, ff)

    nm, hidden, pre_grad, mid_send, mid_keep, t = call(
        mlp_kernel,
        [sds((tok, d)), sds((tok, ff)), sds((tok, ff)), sds(rows2), sds(rows2, F32)],
        (middle, out_grad, w_up, w_down),
        [pltpu.VMEM(rows4, F32)],
    )
    mid_recv = shift(mid_send, "core", 1)

    def image_terms(cols):
        return [sds((2, 4, 80, cols)), sds((4, 80, cols)), sds((4, 80, cols))]

    early_keep, early_a, early_b, order, t = call(
        early_kernel,
        image_terms(2 * ff) + [sds((640, 640))],
        (out_grad, hidden, nm, pre_grad),
        after=t,
    )
    early_ra, early_rb = swap_z(early_a, 0), swap_z(early_b, 1)
    mid_total, mid_total_b, t = call(
        core_sum_kernel, [sds(rows2, F32), sds(rows2)], (mid_keep, mid_recv), after=t
    )
    mid_other = shift(mid_total_b, "yh", 1)
    ni_turned, attended, t = call(
        values_kernel,
        [sds((2, 640, tok)), sds((tok, ev))],
        (inputs, w_value_t, maps_here, order),
        [pltpu.VMEM((tok, d), BF)],
        after=t,
    )
    mid_own, mid_b, t = call(
        mid_kernel,
        [sds((share, d), F32), sds(rows2)],
        (mid_total, mid_other, middle.reshape(rows4), out_grad.reshape(rows4)),
        after=t,
    )
    other_b = shift(mid_b, "core", 1)
    vg, late_keep, late_a, late_b, t = call(
        late_kernel,
        [sds((tok, ev))] + image_terms(2 * ev),
        (mid_b, other_b, maps_here, w_out, attended, ni_turned, order),
        [pltpu.VMEM((tok, d), BF)],
        after=t,
    )
    late_ra, late_rb = swap_z(late_a, 0), swap_z(late_b, 1)
    def over_x(k0, *sends):
        return [k0] + [shift(s, "x", by) for by, s in enumerate(sends, 1)]

    in_send, in_keep, t = call(
        in_part_kernel, [sds(rows2), sds(rows2, F32)], (vg, w_value_t), [pltpu.VMEM(rows4, F32)], after=t
    )
    in_recv = shift(in_send, "core", 1)
    in_own, in_half, t = call(
        in_sum_kernel, [sds((share, d), F32), sds((share, d))], (in_keep, in_recv), after=t
    )
    in_other = shift(in_half, "yh", 1)
    early_own, early_y, t = call(
        add_early_kernel,
        [sds((4, 80, 2 * ff), F32), sds((4, 80, 2 * ff))],
        (early_keep, early_ra, early_rb),
        after=t,
    )
    early_yr = shift(early_y, "yl", 1)
    slab = (2, 80, 2 * ev)
    *late_s, t = call(
        add_late_kernel, [sds(slab, F32)] + [sds(slab)] * 3, (late_keep, late_ra, late_rb), after=t
    )
    late_x = over_x(*late_s)
    slab = (80, 2 * ff)
    *early_s, t = call(
        y_early_kernel, [sds(slab, F32)] + [sds(slab)] * 3, (early_own, early_yr), after=t
    )
    early_x = over_x(*early_s)
    late_own, late_y, t = call(
        two_late_kernel, [sds((80, 2 * ev), F32), sds((80, 2 * ev))], late_x, after=t
    )
    late_yr = shift(late_y, "yl", 1)
    in_grad, t = call(
        in_grad_kernel,
        [sds((share, d))],
        (in_own, in_other, inputs.reshape(rows4), mid_own),
        after=t,
    )
    early_total, t = call(two_early_kernel, [sds(slab, F32)], early_x, after=t)
    cols = 2 * ff + 2 * ev
    own, *sends, t = call(
        two_kernel,
        [sds((20, cols), F32)] + [sds((20, cols))] * 3,
        (early_total, late_own, late_yr),
        [pltpu.VMEM((80, 2 * ev), F32), pltpu.VMEM((4, 20, cols), F32)],
        after=t,
    )
    parts = [shift(block, "zh", by) for by, block in enumerate(sends, 1)]
    grad_down, grad_up, grad_out, grad_value, t = call(
        last_kernel, [sds((20, n), F32) for n in (ff, ff, ev, ev)], (own, *parts), after=t
    )
    return (in_grad, grad_value, grad_out.T, grad_up, grad_down.T)


def solution(mesh):
    split = Mesh(mesh.devices.reshape(2, 4, 4, 2, 2, 2), ("yl", "x", "zh", "zl", "yh", "core"))
    img, head = ("yl", "x", "zh", "zl"), ("yh", "core")
    return jax.shard_map(
        on_device,
        mesh=split,
        in_specs=(
            P(img, None),
            P(img, None),
            P(img, None),
            P(img, head, None, None),
            P(None, head),
            P(head, None),
            P(None, head),
            P(head, None),
        ),
        out_specs=(
            P(img + head, None),
            P(img, head),
            P(head, img),
            P(img, head),
            P(head, img),
        ),
        check_vma=False,
    )
```

```python
import jax
import jax.numpy as jnp
from jax import lax
from jax.experimental import pallas as pl
from jax.experimental.pallas import tpu as pltpu
from jax.sharding import Mesh, PartitionSpec as P

SIZE = {"yl": 2, "x": 4, "zh": 4, "yh": 2, "core": 2}
BF = jnp.bfloat16
F32 = jnp.float32
VM = pl.BlockSpec(memory_space=pltpu.VMEM)
HB = pl.BlockSpec(memory_space=pl.ANY)
MIB = 1024 * 1024
ROOT = 0.7978845608028654
WORK = dict(
    mlp=3e9, early=3e9, core_sum=0, values=1e10, mid=0, late=0, in_part=4e8, in_sum=0, add_early=2e8,
    add_late=0, in_grad=2e8, y_early=0, two_late=2e8, two_early=2e8, two=1e10, last=0,
)


def shift(array, axis, by):
    n = SIZE[axis]
    return lax.ppermute(array, axis, [(i, (i + by) % n) for i in range(n)])


def swap_z(array, first):
    pairs = []
    for i in range(first, 8 + first, 2):
        pairs += [(i % 8, (i + 1) % 8), ((i + 1) % 8, i % 8)]
    return lax.ppermute(array, ("zh", "zl"), pairs)


def dot(a, b, ca, cb):
    return lax.dot_general(a, b, (((ca,), (cb,)), ((), ())), preferred_element_type=F32)


def call(kernel, outs, args, scratch=(), limit=24, after=None):
    n = len(args)
    moved = sum(a.size * a.dtype.itemsize for a in args)
    moved += sum(o.size * o.dtype.itemsize for o in outs)
    tokens = [] if after is None else [after]

    def body(*refs):
        refs = list(refs)
        refs.pop(n + len(tokens) + len(outs))
        pos = [lax.axis_index(a) for a in ("zl", "x", "yh", "core", "yl", "zh")]
        kernel(pos, *refs[:n], *refs[n + len(tokens) :])

    return pl.pallas_call(
        body,
        out_shape=list(outs) + [sds((8, 128), F32)],
        in_specs=[VM] * n + [HB] * len(tokens),
        out_specs=[VM] * len(outs) + [HB],
        scratch_shapes=list(scratch),
        compiler_params=pltpu.CompilerParams(vmem_limit_bytes=limit * MIB),
        cost_estimate=pl.CostEstimate(flops=int(WORK[kernel.__name__.removesuffix('_kernel')]), bytes_accessed=moved, transcendentals=0),
        name=kernel.__name__,
    )(*args, *tokens)


def sds(shape, dtype=BF):
    return jax.ShapeDtypeStruct(shape, dtype)


def norm_parts(rows):
    centre = rows - jnp.mean(rows, axis=-1, keepdims=True)
    factor = lax.rsqrt(jnp.mean(centre * centre, axis=-1, keepdims=True) + 1e-06)
    return centre * factor, factor


def back(rows, grad):
    normed, factor = norm_parts(rows)
    return factor * (
        grad
        - jnp.mean(grad, axis=-1, keepdims=True)
        - normed * jnp.mean(grad * normed, axis=-1, keepdims=True)
    )


def mlp_kernel(pos, middle, out_grad, w_up, w_down, nm, hidden, pre_grad, send, keep, acc):
    core = pos[3]
    width = w_up.shape[1]
    nm[...] = norm_parts(middle[...].astype(F32))[0].astype(BF)
    for lo in range(0, width, 256):
        cols = slice(lo, min(lo + 256, width))
        p = dot(nm[...], w_up[:, cols], 1, 0)
        hg = dot(out_grad[...], w_down[cols, :], 1, 1)
        sq = p * p
        t = jnp.tanh(ROOT * (p * (1.0 + 0.044715 * sq)))
        half = 0.5 * (1.0 + t)
        hidden[:, cols] = (p * half).astype(BF)
        slope = half + 0.5 * p * (1.0 - t * t) * (ROOT * (1.0 + 3 * 0.044715 * sq))
        pre_grad[:, cols] = (slope * hg).astype(BF)
    acc[...] = dot(pre_grad[...], w_up[...], 1, 1).reshape(acc.shape)
    for part in range(2):
        keep[part] = acc[2 * part + core]
        send[part] = acc[2 * part + 1 - core].astype(BF)


def ordering(pos):
    zl, x = pos[0], pos[1]
    new = lax.broadcasted_iota(jnp.int32, (640, 1), 0)
    other, rest = new // 320, new % 320
    parity = zl + other - 2 * zl * other
    by, rest = rest // 80, rest % 80
    z = 2 * (rest // 20) + parity
    old = (x + by) % 4 * 160 + z * 20 + rest % 20
    return (lax.broadcasted_iota(jnp.int32, (640, 640), 1) == old).astype(F32).astype(BF)


def turned(pos, order, a, y):
    at = pl.multiple_of((pos[4] + y - 2 * pos[4] * y) * 640, 640)
    return dot(order[...], a[:, pl.ds(at, 640)], 1, 1).astype(BF)


def put(keep, to, y, at, left, b):
    cols = b.shape[1]
    t = dot(left, b[...], 1, 0).astype(BF).reshape(2, 4, 80, cols)
    keep[y, :, :, at : at + cols] = t[0]
    to[:, :, at : at + cols] = t[1]


def early_kernel(pos, out_grad, hidden, nm, pre_grad, keep, to_a, to_b, order):
    order[...] = ordering(pos)
    cols = hidden.shape[1]
    for y, out in ((0, to_a), (1, to_b)):
        put(keep, out, y, 0, turned(pos, order, out_grad, y), hidden)
        put(keep, out, y, cols, turned(pos, order, nm, y), pre_grad)


def add_early_kernel(pos, keep, from_a, from_b, own, send):
    own[...] = keep[0].astype(F32) + from_a[...].astype(F32)
    send[...] = (keep[1].astype(F32) + from_b[...].astype(F32)).astype(BF)


def y_early_kernel(pos, own, recv, k0, s1, s2, s3):
    for by, out in enumerate((k0, s1, s2, s3)):
        out[...] = (own[by] + recv[by].astype(F32)).astype(out.dtype)


def add_late_kernel(pos, keep, from_a, from_b, k0, s1, s2, s3):
    for y, recv in ((0, from_a), (1, from_b)):
        for by, out in enumerate((k0, s1, s2, s3)):
            total = keep[y, by].astype(F32) + recv[by].astype(F32)
            out[y] = total.astype(out.dtype)


def x_sum(k0, r1, r2, r3):
    return k0[...] + r2[...].astype(F32) + r1[...].astype(F32) + r3[...].astype(F32)


def two_late_kernel(pos, k0, r1, r2, r3, own, send):
    total = x_sum(k0, r1, r2, r3)
    own[...] = total[0]
    send[...] = total[1].astype(BF)


def two_early_kernel(pos, k0, r1, r2, r3, total):
    total[...] = x_sum(k0, r1, r2, r3)


def two_kernel(pos, early, late, recv, *rest):
    *outs, both, cut = rest
    both[...] = late[...] + recv[...].astype(F32)
    cols = early.shape[1]
    for k in range(4):
        cut[k, :, :cols] = early[20 * k : 20 * k + 20]
        cut[k, :, cols:] = both[20 * k : 20 * k + 20]
    for i, out in enumerate(outs):
        out[...] = cut[lax.rem(pos[5] + i, 4)].astype(out.dtype)


def last_kernel(pos, own, *rest):
    parts, outs = rest[:3], rest[3:]
    total = own[...]
    for part in parts:
        total = total + part[...].astype(F32)
    at = 0
    for out in outs:
        cols = out.shape[1]
        out[...] = total[:, at : at + cols]
        at += cols


def by_head(maps, columns, contract):
    heads = maps.shape[0]
    size = columns.shape[1] // heads
    lane = lax.broadcasted_iota(jnp.int32, columns.shape, 1)
    total = None
    for h in range(heads):
        mine = (lane >= h * size) & (lane < (h + 1) * size)
        part = jnp.where(mine, columns, jnp.zeros_like(columns)).astype(BF)
        part = dot(maps[h], part, contract, 0)
        total = part if total is None else total + part
    return total


def values_kernel(pos, inputs, w_value_t, maps, order, ni_turned, attended, ni):
    ni[...] = norm_parts(inputs[...].astype(F32))[0].astype(BF)
    values = dot(ni[...], w_value_t[...], 1, 1).astype(BF).astype(F32)
    attended[...] = by_head(maps, values, 1).astype(BF)
    for y in range(2):
        ni_turned[y] = turned(pos, order, ni, y)


def core_sum_kernel(pos, keep, recv, total, total_b):
    s = keep[...] + recv[...].astype(F32)
    total[...] = s
    total_b[...] = s.astype(BF)


def mid_kernel(pos, total, recv, middle, out_grad, own, mid_b):
    yh, core = pos[2], pos[3]
    for part in range(2):
        rows = middle[2 * part + core].astype(F32)
        grad = total[part] + recv[part].astype(F32)
        mid = out_grad[2 * part + core].astype(F32) + back(rows, grad)
        mid_b[part] = mid.astype(BF)

        @pl.when(yh == part)
        def _():
            own[...] = mid


def late_kernel(
    pos, mid_b, other_b, maps, w_out, attended, ni_turned, order, vg, keep, to_a, to_b, mgb
):
    core = pos[3]
    share = mid_b.shape[1]
    for part in range(2):
        for c, rows in ((core, mid_b), (1 - core, other_b)):
            mgb[pl.ds(pl.multiple_of((2 * part + c) * share, share), share)] = rows[part]
    att = dot(mgb[...], w_out[...], 1, 1).astype(BF).astype(F32)
    vg[...] = by_head(maps, att, 0).astype(BF)
    cols = vg.shape[1]
    for y, out in ((0, to_a), (1, to_b)):
        put(keep, out, y, 0, turned(pos, order, mgb, y), attended)
        put(keep, out, y, cols, ni_turned[y], vg)


def in_part_kernel(pos, vg, w_value_t, send, keep, acc):
    core = pos[3]
    acc[...] = dot(vg[...], w_value_t[...], 1, 0).reshape(acc.shape)
    for part in range(2):
        keep[part] = acc[2 * part + core]
        send[part] = acc[2 * part + 1 - core].astype(BF)


def in_sum_kernel(pos, keep, recv, own, send):
    yh = pos[2]
    own[...] = keep[yh] + recv[yh].astype(F32)
    send[...] = (keep[1 - yh] + recv[1 - yh].astype(F32)).astype(BF)


def in_grad_kernel(pos, own, recv, inputs, mid_own, out):
    row = 2 * pos[2] + pos[3]
    grad = own[...] + recv[...].astype(F32)
    out[...] = (mid_own[...] + back(inputs[row].astype(F32), grad)).astype(BF)


def on_device(inputs, middle, out_grad, cached_maps, w_value, w_out, w_up, w_down):
    tok, d = inputs.shape
    ff, ev = w_up.shape[1], w_value.shape[1]
    share = tok // 4
    maps_here = cached_maps[0]
    w_value_t = w_value.T
    rows4 = (4, share, d)
    rows2 = (2, share, d)
    half = (4, 80, ff)
    slab = (2, 80, ff)

    nm, hidden, pre_grad, mid_send, mid_keep, t = call(
        mlp_kernel,
        [sds((tok, d)), sds((tok, ff)), sds((tok, ff)), sds(rows2), sds(rows2, F32)],
        (middle, out_grad, w_up, w_down),
        [pltpu.VMEM(rows4, F32)],
    )
    mid_recv = shift(mid_send, "core", 1)

    def image_terms(cols):
        return [sds((2, 4, 80, cols)), sds((4, 80, cols)), sds((4, 80, cols))]

    early_keep, early_a, early_b, order, t = call(
        early_kernel,
        image_terms(2 * ff) + [sds((640, 640))],
        (out_grad, hidden, nm, pre_grad),
        after=t,
    )
    early_ra, early_rb = swap_z(early_a, 0), swap_z(early_b, 1)
    mid_total, mid_total_b, t = call(
        core_sum_kernel, [sds(rows2, F32), sds(rows2)], (mid_keep, mid_recv), after=t
    )
    mid_other = shift(mid_total_b, "yh", 1)
    ni_turned, attended, t = call(
        values_kernel,
        [sds((2, 640, tok)), sds((tok, ev))],
        (inputs, w_value_t, maps_here, order),
        [pltpu.VMEM((tok, d), BF)],
        after=t,
    )
    mid_own, mid_b, t = call(
        mid_kernel,
        [sds((share, d), F32), sds(rows2)],
        (mid_total, mid_other, middle.reshape(rows4), out_grad.reshape(rows4)),
        after=t,
    )
    other_b = shift(mid_b, "core", 1)
    vg, late_keep, late_a, late_b, t = call(
        late_kernel,
        [sds((tok, ev))] + image_terms(2 * ev),
        (mid_b, other_b, maps_here, w_out, attended, ni_turned, order),
        [pltpu.VMEM((tok, d), BF)],
        after=t,
    )
    late_ra, late_rb = swap_z(late_a, 0), swap_z(late_b, 1)
    def over_x(k0, *sends):
        return [k0] + [shift(s, "x", by) for by, s in enumerate(sends, 1)]

    in_send, in_keep, t = call(
        in_part_kernel, [sds(rows2), sds(rows2, F32)], (vg, w_value_t), [pltpu.VMEM(rows4, F32)], after=t
    )
    in_recv = shift(in_send, "core", 1)
    in_own, in_half, t = call(
        in_sum_kernel, [sds((share, d), F32), sds((share, d))], (in_keep, in_recv), after=t
    )
    in_other = shift(in_half, "yh", 1)
    early_own, early_y, t = call(
        add_early_kernel,
        [sds((4, 80, 2 * ff), F32), sds((4, 80, 2 * ff))],
        (early_keep, early_ra, early_rb),
        after=t,
    )
    early_yr = shift(early_y, "yl", 1)
    slab = (2, 80, 2 * ev)
    *late_s, t = call(
        add_late_kernel, [sds(slab, F32)] + [sds(slab)] * 3, (late_keep, late_ra, late_rb), after=t
    )
    late_x = over_x(*late_s)
    slab = (80, 2 * ff)
    *early_s, t = call(
        y_early_kernel, [sds(slab, F32)] + [sds(slab)] * 3, (early_own, early_yr), after=t
    )
    early_x = over_x(*early_s)
    late_own, late_y, t = call(
        two_late_kernel, [sds((80, 2 * ev), F32), sds((80, 2 * ev))], late_x, after=t
    )
    late_yr = shift(late_y, "yl", 1)
    in_grad, t = call(
        in_grad_kernel,
        [sds((share, d))],
        (in_own, in_other, inputs.reshape(rows4), mid_own),
        after=t,
    )
    early_total, t = call(two_early_kernel, [sds(slab, F32)], early_x, after=t)
    cols = 2 * ff + 2 * ev
    own, *sends, t = call(
        two_kernel,
        [sds((20, cols), F32)] + [sds((20, cols))] * 3,
        (early_total, late_own, late_yr),
        [pltpu.VMEM((80, 2 * ev), F32), pltpu.VMEM((4, 20, cols), F32)],
        after=t,
    )
    parts = [shift(block, "zh", by) for by, block in enumerate(sends, 1)]
    grad_down, grad_up, grad_out, grad_value, t = call(
        last_kernel, [sds((20, n), F32) for n in (ff, ff, ev, ev)], (own, *parts), after=t
    )
    return (in_grad, grad_value, grad_out.T, grad_up, grad_down.T)


def solution(mesh):
    split = Mesh(mesh.devices.reshape(2, 4, 4, 2, 2, 2), ("yl", "x", "zh", "zl", "yh", "core"))
    img, head = ("yl", "x", "zh", "zl"), ("yh", "core")
    return jax.shard_map(
        on_device,
        mesh=split,
        in_specs=(
            P(img, None),
            P(img, None),
            P(img, None),
            P(img, head, None, None),
            P(None, head),
            P(head, None),
            P(None, head),
            P(head, None),
        ),
        out_specs=(
            P(img + head, None),
            P(img, head),
            P(head, img),
            P(img, head),
            P(head, img),
        ),
        check_vma=False,
    )
```
